32 devices in a mesh: grp: 2 (over x), row: 16 (over z, y, core).
Axes of the slice: x: 2, y: 2, z: 4, core: 2. Of those that a mesh axis runs over, the one named last changes fastest.
Arguments:
- coef: float32 [16384, 128], P(('grp', 'row')), parts along dimension 0, may hold values from -2 to 2
- eri: float32 [128, 3, 12, 128, 128], P(('grp', 'row')), parts along dimension 0, may hold values from -0.3125 to 0.3125
- pair_tile: int32 [128, 3], P(('grp', 'row')), parts along dimension 0, may hold values from 0 to 63, as said below
- live_count: int32 [128], P(('grp', 'row')), parts along dimension 0, may hold values from 1 to 3, as said below
Outputs:
- exchange_band: float32 [128, 5, 128, 128], P(('grp', 'row')), parts along dimension 0
The draws below stay inside these ranges and needn't reach their ends.
There are 2 independent parts, one for each index of `grp`. The reference program is written for one: setup_inputs(seed, part) draws one part's arguments, and reference() takes and returns one part's arrays. A program takes and returns all parts, laid end to end along the dimension named above; each array names one. Nothing has to cross between parts.
Inputs may be any that keep to these rules, and one draw needn't show every extreme that they name: `pair_tile`: within a row the tiles are distinct and each differs from the row's own tile index by at most 2. `live_count`: some tile has all 3 slots live.
All inputs are finite; a program needn't handle non-finite values.
Results may differ from the reference program's by a relative error of at most 0.0001.
Values sent between devices are 32-bit elements; how exact they have to be, the bound alone decides.
A program may use at most 64 MiB of HBM per device.

```python
import jax
import jax.numpy as jnp
from jax import lax

TILE = 128
OCC = 128
AUX = 12
REACH = 2
NPAIR = 3
NB = 64
NBF = 8192


def draw_pair_tile(key, part):
    key = jax.random.fold_in(key, 11)
    width = 2 * REACH + 1
    shifts = jnp.arange(width, dtype=jnp.int32) - REACH
    tile_index = jnp.arange(NB, dtype=jnp.int32)[:, None] + shifts[None, :]
    scores = jax.random.randint(key, (NB, width), 0, 1000) * 64 + jnp.arange(width, dtype=jnp.int32)[None, :]
    scores = jnp.where((tile_index >= 0) & (tile_index < NB), scores, 1 << 30)
    ordering = jnp.argsort(scores, axis=1, stable=True)[:, :NPAIR]
    return jnp.take_along_axis(tile_index, ordering, axis=1).astype(jnp.int32)


def draw_live_count(key, part):
    key = jax.random.fold_in(key, 23)
    first_key, second_key = jax.random.split(key)
    counts = jax.random.randint(first_key, (NB,), 1, NPAIR + 1)
    chosen = jax.random.randint(second_key, (), 0, NB)
    return jnp.where(jnp.arange(NB) == chosen, NPAIR, counts).astype(jnp.int32)


def level_of(own_key, shape, pieces, least, top_value):
    loudness, own = 1.0, jax.random.fold_in(own_key, 6)
    for axis_at, parts in pieces:
        heights = jnp.exp(jax.random.uniform(jax.random.fold_in(own, axis_at), (parts,), jnp.float32, least / len(pieces), top_value / len(pieces)))
        loudness = loudness * jnp.repeat(heights, shape[axis_at] // parts).reshape([-1 if axis == axis_at else 1 for axis in range(len(shape))])
    return loudness


def bell_draw(key, shape, spread, reach, cuts=(), held_as=jnp.bfloat16):
    values = jax.random.normal(key, shape, jnp.float32) * spread
    if len(cuts) > 0:
        values = level_of(key, shape, cuts, -0.22, 0.18) * values
    return jnp.clip(values, min=-reach, max=reach).astype(held_as)


def setup_inputs(seed: int = 0, part: int = 0) -> dict:
    key_of = jax.random.split(jax.random.key(seed), 5)
    own_keys = jax.random.split(jax.random.fold_in(key_of[4], part), 5)
    return {
        "coef": bell_draw(own_keys[0], (NBF, OCC), 0.15, 2.0, ((0, 16),), jnp.float32),
        "eri": bell_draw(own_keys[1], (NB, NPAIR, AUX, TILE, TILE), (NPAIR * TILE) ** -0.5, 0.3125, ((0, 16),), jnp.float32),
        "pair_tile": draw_pair_tile(jax.random.fold_in(jax.random.fold_in(key_of[4], part), 71), part),
        "live_count": draw_live_count(jax.random.fold_in(jax.random.fold_in(key_of[4], part), 71), part),
    }


def reference(coef, eri, pair_tile, live_count):
    coef_tiles = coef.reshape(NB, TILE, OCC)
    picked = coef_tiles[pair_tile]
    alive_mask = (jnp.arange(NPAIR, dtype=jnp.int32)[None, :] < live_count[:, None]).astype(coef.dtype)
    picked = picked * alive_mask[:, :, None, None]
    half_done = jnp.einsum('tpqmn,tpni->tqmi', eri, picked, precision=lax.Precision.HIGHEST)
    padded = jnp.pad(half_done, ((REACH, REACH), (0, 0), (0, 0), (0, 0)))
    band_tiles = []
    for offset in range(2 * REACH + 1):
        partner = padded[offset:offset + NB]
        band_tiles.append(jnp.einsum('tqmi,tqni->tmn', half_done, partner, precision=lax.Precision.HIGHEST))
    return jnp.stack(band_tiles, axis=1)
```

```python
import functools

import jax
import jax.numpy as jnp
from jax import lax
from jax.experimental import pallas as pl
from jax.experimental.pallas import tpu as pltpu
from jax.sharding import PartitionSpec as P

REACH = 2
STEP = 2
MESH = pl.DeviceIdType.MESH
F32, BF16 = jnp.float32, jnp.bfloat16


def split(x):
    high = x.astype(BF16)
    return high, (x - high.astype(F32)).astype(BF16)


def nt(left, right):
    return lax.dot_general(left, right, (((1,), (1,)), ((), ())), preferred_element_type=F32)


def kernel(
    ndev, pair_ref, live_ref, coef_ref, eri_ref, out_ref,
    cext, eri_v, parts, weights, h_hi, h_lo, snd, rcv, acc, ksnd, out_v,
    coef_sem, eri_sem, csend, crecv, hsend, hrecv, ksend, krecv, early_sem, late_sem,
):
    tiles, slots, aux, wide, _ = eri_v.shape
    orb = cext.shape[-1]
    span = slots * wide
    chunks = aux // STEP
    last = tiles - 1
    grp, row = lax.axis_index("grp"), lax.axis_index("row")
    has = (row > 0, row < ndev - 1)
    peer = ((grp, row - 1), (grp, row + 1))
    edge = (0, last)

    def remote(src, dst, send, recv, side):
        return pltpu.make_async_remote_copy(
            src_ref=src, dst_ref=dst, send_sem=send, recv_sem=recv,
            device_id=peer[side], device_id_type=MESH,
        )

    load = pltpu.make_async_copy(coef_ref, cext.at[pl.ds(REACH, tiles)], coef_sem)
    load.start()
    order = (last, 0) + tuple(range(1, last))
    loads = [pltpu.make_async_copy(eri_ref.at[t], eri_v.at[t], eri_sem.at[t]) for t in range(tiles)]
    for t in order:
        loads[t].start()

    barrier = pltpu.get_barrier_semaphore()
    for side in (0, 1):
        @pl.when(has[side])
        def _():
            pl.semaphore_signal(barrier, inc=1, device_id=peer[side], device_id_type=MESH)
    pl.semaphore_wait(barrier, has[0].astype(jnp.int32) + has[1].astype(jnp.int32))
    load.wait()

    def coef_copy(side):
        src = (REACH, tiles)[side]
        dst = (REACH + tiles, 0)[side]
        return remote(
            cext.at[pl.ds(src, REACH)], cext.at[pl.ds(dst, REACH)],
            csend.at[side], crecv.at[1 - side], side,
        )

    for side in (1, 0):
        @pl.when(has[side])
        def _():
            coef_copy(side).start()

        @pl.when(jnp.logical_not(has[side]))
        def _():
            rcv[side] = jnp.zeros(rcv.shape[1:], F32)
            cext[pl.ds((0, REACH + tiles)[side], REACH)] = jnp.zeros((REACH, wide, orb), F32)
            out_v[edge[side], (0, 2 * REACH)[side]] = jnp.zeros((wide, wide), F32)

    def split_eri(t):
        loads[t].wait()

        def body(q, carry):
            for p in range(slots):
                high, low = split(eri_v[t, p, q])
                parts[t, q, :, p * wide:(p + 1) * wide] = high
                parts[t, q, :, span + p * wide:span + (p + 1) * wide] = low
            return carry

        lax.fori_loop(0, aux, body, 0)

    def pick(t):
        live = live_ref[t]
        for p in range(slots):
            index = jnp.clip(pair_ref[t, p] - row * tiles + REACH, 0, tiles + 2 * REACH - 1)
            high, low = split(jnp.where(p < live, cext[index], 0.0))
            both = jnp.concatenate([high, low], axis=1)
            weights[t, p * wide:(p + 1) * wide, :] = both
            weights[t, span + p * wide:span + (p + 1) * wide, :] = both

    def half(t, first, count, side=None):
        left = parts[t, first:first + count].reshape(count * wide, 2 * span)
        both = jnp.dot(left, weights[t], preferred_element_type=F32)
        block = both[:, :orb] + both[:, orb:]
        for k in range(count):
            x = block[k * wide:(k + 1) * wide]
            high, low = split(x)
            rows, cols = slice(t * wide, (t + 1) * wide), slice((first + k) * orb, (first + k + 1) * orb)
            h_hi[rows, cols] = high
            h_lo[rows, cols] = low
            if side is not None:
                snd[side, first + k] = x

    split_eri(last)
    split_eri(0)
    for side in (0, 1):
        @pl.when(has[side])
        def _():
            coef_copy(1 - side).wait_recv()
    pick(last)
    pick(0)

    def half_copy(side, c):
        piece = pl.ds(c * STEP, STEP)
        return remote(
            snd.at[side, piece], rcv.at[1 - side, piece],
            hsend.at[side, c], hrecv.at[1 - side, c], side,
        )

    for c in range(chunks):
        for side in (1, 0):
            half(edge[side], c * STEP, STEP, side)

            @pl.when(has[side])
            def _():
                half_copy(side, c).start()

    for t in range(1, last):
        split_eri(t)
        pick(t)
        for c in range(2):
            half(t, c * (aux // 2), aux // 2)

    for first in range(0, tiles, 2):
        rows = pl.ds(first * wide, 2 * wide)
        gram = nt(h_hi[...], h_hi[rows, :]) + nt(h_lo[...], h_hi[rows, :]) + nt(h_hi[...], h_lo[rows, :])
        for other in (first, first + 1):
            for t in range(max(0, other - REACH), min(tiles, other + REACH + 1)):
                col = (other - first) * wide
                out_v[t, other - t + REACH] = gram[t * wide:(t + 1) * wide, col:col + wide]

    early = []
    for t in range(tiles):
        low, high = max(0, REACH - t), min(2 * REACH, tiles - 1 - t + REACH)
        piece = pl.ds(low, high - low + 1)
        early.append(pltpu.make_async_copy(out_v.at[t, piece], out_ref.at[t, piece], early_sem.at[t]))
        early[-1].start()

    acc[...] = jnp.zeros_like(acc)
    near = (pl.ds(0, 2 * wide), pl.ds((tiles - 2) * wide, 2 * wide))
    for c in range(chunks):
        for side in (0, 1):
            @pl.when(has[side])
            def _():
                half_copy(1 - side, c).wait_recv()
            cols = pl.ds(c * STEP * orb, STEP * orb)
            x = jnp.concatenate([rcv[side, c * STEP + k] for k in range(STEP)], axis=1)
            high, low = split(x)
            mine = h_hi[near[side], cols]
            acc[side] += nt(high, mine) + nt(low, mine) + nt(high, h_lo[near[side], cols])

    far = (slice(wide, 2 * wide), slice(0, wide))
    close = (slice(0, wide), slice(wide, 2 * wide))
    far_tile = (1, tiles - 2)
    far_at = (0, 2 * REACH)

    def k_copy(side):
        return remote(
            ksnd.at[side], out_ref.at[edge[1 - side], far_at[1 - side]],
            ksend.at[side], krecv.at[1 - side], side,
        )

    late = []
    for side in (0, 1):
        ksnd[side] = acc[side, :, far[side]]

        @pl.when(has[side])
        def _():
            k_copy(side).start()
    for side in (0, 1):
        out_v[far_tile[side], far_at[side]] = acc[side, :, far[side]].T
        out_v[edge[side], (1, 3)[side]] = acc[side, :, close[side]].T
        for n, (t, o) in enumerate(((far_tile[side], far_at[side]), (edge[side], (1, 3)[side]))):
            late.append(pltpu.make_async_copy(out_v.at[t, o], out_ref.at[t, o], late_sem.at[side, n]))
            late[-1].start()

        @pl.when(jnp.logical_not(has[side]))
        def _():
            fill = pltpu.make_async_copy(
                out_v.at[edge[side], far_at[side]], out_ref.at[edge[side], far_at[side]], krecv.at[side]
            )
            fill.start()
            fill.wait()

    for copy in early + late:
        copy.wait()
    for side in (0, 1):
        @pl.when(has[side])
        def _():
            coef_copy(side).wait_send()
            for c in range(chunks):
                half_copy(side, c).wait_send()
            k_copy(side).wait_send()
            k_copy(1 - side).wait_recv()


def on_device(ndev, coef, eri, pair_tile, live_count):
    tiles, slots, aux, wide, _ = eri.shape
    orb = coef.shape[1]
    chunks = aux // STEP
    dma = pltpu.SemaphoreType.DMA
    flops = 2 * 3 * tiles * aux * wide * wide * orb * (slots + 2 * REACH + 1)
    return pl.pallas_call(
        functools.partial(kernel, ndev),
        out_shape=jax.ShapeDtypeStruct((tiles, 2 * REACH + 1, wide, wide), F32),
        in_specs=[
            pl.BlockSpec(memory_space=pltpu.SMEM),
            pl.BlockSpec(memory_space=pltpu.SMEM),
            pl.BlockSpec(memory_space=pl.ANY),
            pl.BlockSpec(memory_space=pl.ANY),
        ],
        out_specs=pl.BlockSpec(memory_space=pl.ANY),
        scratch_shapes=[
            pltpu.VMEM((tiles + 2 * REACH, wide, orb), F32),
            pltpu.VMEM(eri.shape, F32),
            pltpu.VMEM((tiles, aux, wide, 2 * slots * wide), BF16),
            pltpu.VMEM((tiles, 2 * slots * wide, 2 * orb), BF16),
            pltpu.VMEM((tiles * wide, aux * orb), BF16),
            pltpu.VMEM((tiles * wide, aux * orb), BF16),
            pltpu.VMEM((2, aux, wide, orb), F32),
            pltpu.VMEM((2, aux, wide, orb), F32),
            pltpu.VMEM((2, wide, 2 * wide), F32),
            pltpu.VMEM((2, wide, wide), F32),
            pltpu.VMEM((tiles, 2 * REACH + 1, wide, wide), F32),
            dma(()), dma((tiles,)), dma((2,)), dma((2,)), dma((2, chunks)), dma((2, chunks)),
            dma((2,)), dma((2,)), dma((tiles,)), dma((2, 2)),
        ],
        compiler_params=pltpu.CompilerParams(
            collective_id=0, has_side_effects=True, vmem_limit_bytes=50 * 2**20
        ),
        cost_estimate=pl.CostEstimate(
            flops=flops, bytes_accessed=4 * eri.size, transcendentals=0
        ),
    )(pair_tile, live_count, coef.reshape(tiles, wide, orb), eri)


def solution(mesh):
    return jax.shard_map(
        functools.partial(on_device, mesh.shape["row"]),
        mesh=mesh,
        in_specs=(
            P(("grp", "row"), None),
            P(("grp", "row"), None, None, None, None),
            P(("grp", "row"), None),
            P(("grp", "row")),
        ),
        out_specs=P(("grp", "row"), None, None, None),
        check_vma=False,
    )
```

```python
import functools

import jax
import jax.numpy as jnp
from jax import lax
from jax.experimental import pallas as pl
from jax.experimental.pallas import tpu as pltpu
from jax.sharding import PartitionSpec as P

REACH = 2
STEP = 2
DEPTH = 2
MESH = pl.DeviceIdType.MESH
F32, BF16 = jnp.float32, jnp.bfloat16


def split(x):
    high = x.astype(BF16)
    return high, (x - high.astype(F32)).astype(BF16)


def nt(left, right):
    return lax.dot_general(left, right, (((1,), (1,)), ((), ())), preferred_element_type=F32)


def kernel(
    ndev, pair_hbm, live_hbm, coef_ref, eri_ref, out_ref,
    pair_ref, live_ref, cext, eri_v, parts, weights, h_hi, h_lo, snd, rcv, acc, ksnd, out_v,
    index_sem, coef_sem, eri_sem, csend, crecv, hsend, hrecv, ksend, krecv, early_sem, late_sem,
):
    tiles, slots, aux, wide, _ = eri_v.shape
    orb = cext.shape[-1]
    span = slots * wide
    chunks = aux // STEP
    last = tiles - 1
    grp, row = lax.axis_index("grp"), lax.axis_index("row")
    has = (row > 0, row < ndev - 1)
    peer = ((grp, row - 1), (grp, row + 1))
    edge = (0, last)

    def remote(src, dst, send, recv, side):
        return pltpu.make_async_remote_copy(
            src_ref=src, dst_ref=dst, send_sem=send, recv_sem=recv,
            device_id=peer[side], device_id_type=MESH,
        )

    load = pltpu.make_async_copy(coef_ref, cext.at[pl.ds(REACH, tiles)], coef_sem)
    load.start()
    small = (
        pltpu.make_async_copy(pair_hbm, pair_ref, index_sem.at[0]),
        pltpu.make_async_copy(live_hbm, live_ref, index_sem.at[1]),
    )
    for copy in small:
        copy.start()
    order = (last, 0) + tuple(range(1, last))
    loads = [pltpu.make_async_copy(eri_ref.at[t], eri_v.at[t], eri_sem.at[t]) for t in range(tiles)]
    for t in order:
        loads[t].start()

    barrier = pltpu.get_barrier_semaphore()
    for side in (0, 1):
        @pl.when(has[side])
        def _():
            pl.semaphore_signal(barrier, inc=1, device_id=peer[side], device_id_type=MESH)
    pl.semaphore_wait(barrier, has[0].astype(jnp.int32) + has[1].astype(jnp.int32))
    load.wait()

    def coef_copy(side):
        src = (REACH, tiles)[side]
        dst = (REACH + tiles, 0)[side]
        return remote(
            cext.at[pl.ds(src, REACH)], cext.at[pl.ds(dst, REACH)],
            csend.at[side], crecv.at[1 - side], side,
        )

    for side in (1, 0):
        @pl.when(has[side])
        def _():
            coef_copy(side).start()

        @pl.when(jnp.logical_not(has[side]))
        def _():
            rcv[side] = jnp.zeros(rcv.shape[1:], F32)
            cext[pl.ds((0, REACH + tiles)[side], REACH)] = jnp.zeros((REACH, wide, orb), F32)
            out_v[edge[side], (0, 2 * REACH)[side]] = jnp.zeros((wide, wide), F32)

    def split_eri(t):
        loads[t].wait()

        def body(q, carry):
            for p in range(slots):
                high, low = split(eri_v[t, p, q])
                parts[t, q, :, p * wide:(p + 1) * wide] = high
                parts[t, q, :, span + p * wide:span + (p + 1) * wide] = low
            return carry

        lax.fori_loop(0, aux, body, 0)

    def pick(t):
        live = live_ref[t]
        for p in range(slots):
            index = jnp.clip(pair_ref[t, p] - row * tiles + REACH, 0, tiles + 2 * REACH - 1)
            high, low = split(jnp.where(p < live, cext[index], 0.0))
            both = jnp.concatenate([high, low], axis=1)
            weights[t, p * wide:(p + 1) * wide, :] = both
            weights[t, span + p * wide:span + (p + 1) * wide, :] = both

    def half(t, first, count, side=None):
        left = parts[t, first:first + count].reshape(count * wide, 2 * span)
        both = jnp.dot(left, weights[t], preferred_element_type=F32)
        block = both[:, :orb] + both[:, orb:]
        for k in range(count):
            x = block[k * wide:(k + 1) * wide]
            high, low = split(x)
            rows, cols = slice(t * wide, (t + 1) * wide), slice((first + k) * orb, (first + k + 1) * orb)
            h_hi[rows, cols] = high
            h_lo[rows, cols] = low
            if side is not None:
                snd[side, first + k] = x

    split_eri(last)
    split_eri(0)
    for copy in small:
        copy.wait()
    for side in (0, 1):
        @pl.when(has[side])
        def _():
            coef_copy(1 - side).wait_recv()
    pick(last)
    pick(0)

    def half_copy(side, c):
        piece = pl.ds(c * STEP, STEP)
        return remote(
            snd.at[side, piece], rcv.at[1 - side, piece],
            hsend.at[side, c], hrecv.at[1 - side, c], side,
        )

    def pump(c):
        for side in (1, 0):
            @pl.when(has[side])
            def _():
                if c >= DEPTH:
                    half_copy(side, c - DEPTH).wait_send()
                half_copy(side, c).start()

    for c in range(DEPTH):
        for side in (1, 0):
            half(edge[side], c * STEP, STEP, side)
        pump(c)
    done = DEPTH * STEP
    for side in (1, 0):
        half(edge[side], done, aux - done, side)

    split_eri(1)
    pick(1)
    half(1, 0, aux)
    pump(DEPTH)
    for t in range(2, last):
        split_eri(t)
        pick(t)
        half(t, 0, aux)

    for first in range(0, tiles, 2):
        rows = pl.ds(first * wide, 2 * wide)
        gram = nt(h_hi[...], h_hi[rows, :]) + nt(h_lo[...], h_hi[rows, :]) + nt(h_hi[...], h_lo[rows, :])
        for other in (first, first + 1):
            for t in range(max(0, other - REACH), min(tiles, other + REACH + 1)):
                col = (other - first) * wide
                out_v[t, other - t + REACH] = gram[t * wide:(t + 1) * wide, col:col + wide]
        if first == 0:
            pump(DEPTH + 1)

    early = []
    for t in range(tiles):
        low, high = max(0, REACH - t), min(2 * REACH, tiles - 1 - t + REACH)
        piece = pl.ds(low, high - low + 1)
        early.append(pltpu.make_async_copy(out_v.at[t, piece], out_ref.at[t, piece], early_sem.at[t]))
        early[-1].start()

    acc[...] = jnp.zeros_like(acc)
    near = (pl.ds(0, 2 * wide), pl.ds((tiles - 2) * wide, 2 * wide))
    for c in range(chunks):
        if c + DEPTH + 2 < chunks:
            pump(c + DEPTH + 2)
        for side in (0, 1):
            @pl.when(has[side])
            def _():
                half_copy(1 - side, c).wait_recv()
            cols = pl.ds(c * STEP * orb, STEP * orb)
            x = jnp.concatenate([rcv[side, c * STEP + k] for k in range(STEP)], axis=1)
            high, low = split(x)
            mine = h_hi[near[side], cols]
            both = nt(jnp.concatenate([high, low], axis=0), mine)
            acc[side] += both[:wide] + both[wide:] + nt(high, h_lo[near[side], cols])

    far = (slice(wide, 2 * wide), slice(0, wide))
    close = (slice(0, wide), slice(wide, 2 * wide))
    far_tile = (1, tiles - 2)
    far_at = (0, 2 * REACH)

    def k_copy(side):
        return remote(
            ksnd.at[side], out_ref.at[edge[1 - side], far_at[1 - side]],
            ksend.at[side], krecv.at[1 - side], side,
        )

    late = []
    for side in (0, 1):
        ksnd[side] = acc[side, :, far[side]]

        @pl.when(has[side])
        def _():
            k_copy(side).start()
    for side in (0, 1):
        out_v[far_tile[side], far_at[side]] = acc[side, :, far[side]].T
        out_v[edge[side], (1, 3)[side]] = acc[side, :, close[side]].T
        for n, (t, o) in enumerate(((far_tile[side], far_at[side]), (edge[side], (1, 3)[side]))):
            late.append(pltpu.make_async_copy(out_v.at[t, o], out_ref.at[t, o], late_sem.at[side, n]))
            late[-1].start()

        @pl.when(jnp.logical_not(has[side]))
        def _():
            fill = pltpu.make_async_copy(
                out_v.at[edge[side], far_at[side]], out_ref.at[edge[side], far_at[side]], krecv.at[side]
            )
            fill.start()
            fill.wait()

    for copy in early + late:
        copy.wait()
    for side in (0, 1):
        @pl.when(has[side])
        def _():
            coef_copy(side).wait_send()
            for c in range(chunks - DEPTH, chunks):
                half_copy(side, c).wait_send()
            k_copy(side).wait_send()
            k_copy(1 - side).wait_recv()


def on_device(ndev, coef, eri, pair_tile, live_count):
    tiles, slots, aux, wide, _ = eri.shape
    orb = coef.shape[1]
    chunks = aux // STEP
    dma = pltpu.SemaphoreType.DMA
    flops = 2 * 3 * tiles * aux * wide * wide * orb * (slots + 2 * REACH + 1)
    return pl.pallas_call(
        functools.partial(kernel, ndev),
        out_shape=jax.ShapeDtypeStruct((tiles, 2 * REACH + 1, wide, wide), F32),
        in_specs=[
            pl.BlockSpec(memory_space=pltpu.HBM),
            pl.BlockSpec(memory_space=pltpu.HBM),
            pl.BlockSpec(memory_space=pltpu.HBM),
            pl.BlockSpec(memory_space=pltpu.HBM),
        ],
        out_specs=pl.BlockSpec(memory_space=pl.ANY),
        scratch_shapes=[
            pltpu.SMEM(pair_tile.shape, jnp.int32),
            pltpu.SMEM(live_count.shape, jnp.int32),
            pltpu.VMEM((tiles + 2 * REACH, wide, orb), F32),
            pltpu.VMEM(eri.shape, F32),
            pltpu.VMEM((tiles, aux, wide, 2 * slots * wide), BF16),
            pltpu.VMEM((tiles, 2 * slots * wide, 2 * orb), BF16),
            pltpu.VMEM((tiles * wide, aux * orb), BF16),
            pltpu.VMEM((tiles * wide, aux * orb), BF16),
            pltpu.VMEM((2, aux, wide, orb), F32),
            pltpu.VMEM((2, aux, wide, orb), F32),
            pltpu.VMEM((2, wide, 2 * wide), F32),
            pltpu.VMEM((2, wide, wide), F32),
            pltpu.VMEM((tiles, 2 * REACH + 1, wide, wide), F32),
            dma((2,)), dma(()), dma((tiles,)), dma((2,)), dma((2,)), dma((2, chunks)), dma((2, chunks)),
            dma((2,)), dma((2,)), dma((tiles,)), dma((2, 2)),
        ],
        compiler_params=pltpu.CompilerParams(
            collective_id=0, has_side_effects=True, vmem_limit_bytes=50 * 2**20
        ),
        cost_estimate=pl.CostEstimate(
            flops=flops, bytes_accessed=4 * eri.size, transcendentals=0
        ),
    )(pair_tile, live_count, coef.reshape(tiles, wide, orb), eri)


def solution(mesh):
    return jax.shard_map(
        functools.partial(on_device, mesh.shape["row"]),
        mesh=mesh,
        in_specs=(
            P(("grp", "row"), None),
            P(("grp", "row"), None, None, None, None),
            P(("grp", "row"), None),
            P(("grp", "row")),
        ),
        out_specs=P(("grp", "row"), None, None, None),
        check_vma=False,
    )
```
